1024 devices in a mesh: context: 64 (over x, z_lo), tensor: 16 (over z_hi, y, core).
Axes of the slice: x: 4, y: 4, z: 32 (z_hi: 2, z_lo: 16; z = z_hi * 16 + z_lo), core: 2. Of those that a mesh axis runs over, the one named last changes fastest.
Arguments:
- streams: bfloat16 [4096, 3, 8192], P('tensor', None, 'context'), may hold values from -6 to 6
- out_weight: bfloat16 [4096, 8192], P(None, 'tensor'), may hold values from -0.09375 to 0.09375
- cotangent: bfloat16 [8192, 8192], P('context', 'tensor'), may hold values from -6 to 6
- residues: float32 [4096, 16], P(('tensor', 'context')), may hold values from -0.0625 to 0.0625
- decay_rates: float32 [4096, 16], P(('tensor', 'context')), may hold values from 0.5 to 273
- skip_gain: float32 [4096], P(('tensor', 'context')), may hold values from 0.5 to 1.5
Outputs:
- block_out: float32 [8192, 8192], P('context', 'tensor')
- proj_grad: float32 [4096, 3, 8192], P('tensor', None, 'context')
- residue_grad: float32 [4096, 16], P(('tensor', 'context'))
- decay_grad: float32 [4096, 16], P(('tensor', 'context'))
- skip_grad: float32 [4096], P(('tensor', 'context'))
The draws below stay inside these ranges and needn't reach their ends.
All inputs are finite; a program needn't handle non-finite values.
Results may differ from the reference program's by a relative error of at most 0.0029.
Values may be sent and summed in bfloat16 or wider, within the bound.
A program may use at most 32 MiB of HBM per device.

```python
import math
import jax
import jax.numpy as jnp
from jax import lax

D = 8192
ORDER = 16
SEQ = 8192
CH = 4096


def block_levels(rng, extent, split, smallest, high):
    loudness, own = 1.0, jax.random.fold_in(rng, 6)
    for position, blocks in split:
        steps = jnp.exp(jax.random.uniform(jax.random.fold_in(own, position), (blocks,), jnp.float32, smallest / len(split), high / len(split)))
        loudness = loudness * jnp.repeat(steps, extent[position] // blocks).reshape([-1 if axis == position else 1 for axis in range(len(extent))])
    return loudness


def noise(stream_key, shape, scale, most, split=(), held_as=jnp.bfloat16):
    loudness = block_levels(stream_key, shape, split, -0.22, 0.18) if split else 1.0
    values = jax.random.normal(stream_key, shape, jnp.float32) * scale * loudness
    return jnp.minimum(jnp.maximum(values, -most), most).astype(held_as)


def setup_inputs(seed: int = 0) -> dict:
    seeds = jax.random.split(jax.random.key(seed), 7)
    streams = noise(seeds[0], (CH, 3, SEQ), 1.0, 6.0, ((0, 16), (2, 64)))
    out_weight = noise(seeds[1], (CH, D), CH ** -0.5, 0.09375, ((1, 16),))
    cotangent = noise(seeds[2], (SEQ, D), 1.0, 6.0, ((0, 64), (1, 16)))
    residues = noise(seeds[3], (CH, ORDER), SEQ ** -0.5, 0.0625, ((0, 1024),), jnp.float32)
    decay_rates = jnp.clip(jnp.exp(math.log(273.0) - 6.302619 * jax.random.uniform(seeds[4], (CH, ORDER), jnp.float32) ** block_levels(seeds[4], (CH, ORDER), ((0, 1024),), -0.2, 0.2)), 0.5, 273.0)
    skip_gain = jnp.clip(0.5 + 1.0 * jax.random.uniform(seeds[5], (CH,), jnp.float32) ** block_levels(seeds[5], (CH,), ((0, 1024),), -0.2, 0.2), 0.5, 1.5)
    return dict(streams=streams, out_weight=out_weight, cotangent=cotangent, residues=residues, decay_rates=decay_rates, skip_gain=skip_gain)


HIGHEST_PRECISION = lax.Precision.HIGHEST


def channel_work(operands):
    product_row, grad_row, residue_row, decay_row, skip_value = operands
    fft_len = 2 * SEQ
    positions = jnp.arange(SEQ, dtype=jnp.float32) / SEQ
    decays = jnp.exp(-decay_row[:, None] * positions[None, :])
    filter_row = jnp.dot(residue_row, decays, precision=HIGHEST_PRECISION)
    spec_mix = jnp.fft.rfft(product_row, fft_len)
    spec_filter = jnp.fft.rfft(filter_row, fft_len)
    spec_grad = jnp.fft.rfft(grad_row, fft_len)
    conv_row = jnp.fft.irfft(spec_mix * spec_filter, fft_len)[:SEQ] + skip_value * product_row
    back_row = jnp.fft.irfft(jnp.conj(spec_filter) * spec_grad, fft_len)[:SEQ] + skip_value * grad_row
    filter_grad = jnp.fft.irfft(jnp.conj(spec_mix) * spec_grad, fft_len)[:SEQ]
    residue_grad = jnp.dot(decays, filter_grad, precision=HIGHEST_PRECISION)
    decay_grad = -residue_row * jnp.dot(decays, filter_grad * positions, precision=HIGHEST_PRECISION)
    skip_grad = jnp.sum(grad_row * product_row)
    return conv_row, back_row, residue_grad, decay_grad, skip_grad


def reference(streams, out_weight, cotangent, residues, decay_rates, skip_gain):
    projected = streams.astype(jnp.float32)
    query_rows = projected[:, 0]
    key_rows = projected[:, 1]
    value_rows = projected[:, 2]
    product_rows = key_rows * value_rows
    grad_gated = jnp.dot(out_weight, cotangent.T, preferred_element_type=jnp.float32)
    grad_conv = grad_gated * query_rows
    conv_rows, back_rows, residue_grad, decay_grad, skip_grad = lax.map(channel_work, (product_rows, grad_conv, residues, decay_rates, skip_gain))
    gated = (query_rows * conv_rows).astype(jnp.bfloat16)
    block_out = jnp.dot(gated.T, out_weight, preferred_element_type=jnp.float32)
    proj_grad = jnp.stack([grad_gated * conv_rows, back_rows * value_rows, back_rows * key_rows], axis=1)
    return block_out, proj_grad, residue_grad, decay_grad, skip_grad
```

```python
import functools

import jax
import jax.numpy as jnp
from jax import lax
from jax.experimental import pallas as pl
from jax.experimental.pallas import tpu as pltpu
from jax.sharding import PartitionSpec as P

MESH = pl.DeviceIdType.MESH
F32, BF16 = jnp.float32, jnp.bfloat16
HIGHEST = lax.Precision.HIGHEST
SEQ = 8192.0
CTX = 64
CHUNK = 128
SUB, STEPS = 8, 16
LANES = 128
GROUPS = 2
OWNERS = 4
OROWS = 8
GROWS = 24


def owner_of(o):
    return o * 16 + 7 + o % 2


def remote(src, dst, send, recv, device):
    return pltpu.make_async_remote_copy(
        src_ref=src, dst_ref=dst, send_sem=send, recv_sem=recv, device_id=device, device_id_type=MESH
    )


def dot(a, b):
    return jnp.dot(a, b, preferred_element_type=F32)


def dot_nt(a, b):
    return lax.dot_general(a, b, (((1,), (1,)), ((), ())), preferred_element_type=F32)


def kernel(
    res_hbm, dec_hbm, skip_hbm, qkv_hbm, cot_hbm, w_hbm,
    out_ref, proj_ref, res_ref, dec_ref, skip_ref,
    res_in, dec_in, skip_in, qkv_in, cot_in, w_ref,
    packed, g_all, g_two, psend, pown, prx, ysend, yrx, zsend, zrx,
    etx, erx, stx, sin, btx, brx, otx, bin_, gtx, grx, gsum, frx, ktx, krx, ksum, kfin,
    a_t, r_t, f_t, v_t, a16_t, ek_t, bk_t, a128_t, skip_t,
    qs, ks, vs, mix, grad, gconv, conv, back, turn, gall,
    sem_s, sem_r, ag_s, ag_r, sem_l,
):
    me = lax.axis_index("context")
    tensor = lax.axis_index("tensor")
    zh, y, c = tensor // 8, (tensor // 2) % 4, tensor % 2

    def at(zh_, y_, c_):
        return zh_ * 8 + y_ * 2 + c_

    def tdev(zh_, y_, c_):
        return (me, at(zh_, y_, c_))

    def cdev(j):
        return (j, tensor)

    ys = [lax.rem(y + d, 4) for d in range(4)]
    barrier = pltpu.get_barrier_semaphore()

    @pl.loop(1, CTX)
    def _(i):
        pl.semaphore_signal(barrier, inc=1, device_id=cdev(lax.rem(me + i, CTX)), device_id_type=MESH)

    for device in [tdev(1 - zh, y, c), tdev(zh, y, 1 - c)] + [tdev(zh, ys[d], c) for d in (1, 2, 3)]:
        pl.semaphore_signal(barrier, inc=1, device_id=device, device_id_type=MESH)

    loads = [
        pltpu.make_async_copy(src, dst, sem_l.at[k])
        for k, (src, dst) in enumerate(
            [(res_hbm, res_in), (dec_hbm, dec_in), (skip_hbm, skip_in), (cot_hbm, cot_in), (w_hbm, w_ref), (qkv_hbm, qkv_in)]
        )
    ]
    for load in loads:
        load.start()
    for load in loads[:3]:
        load.wait()
    lane = lax.broadcasted_iota(jnp.int32, (16, LANES), 1) % 32
    mode = lax.broadcasted_iota(jnp.int32, (16, LANES), 0)
    spread = jnp.dot(
        res_in[...], jnp.where(lane == mode, 1.0, 0.0).astype(F32), precision=HIGHEST, preferred_element_type=F32
    ) + jnp.dot(
        dec_in[...], jnp.where(lane == mode + 16, 1.0, 0.0).astype(F32), precision=HIGHEST, preferred_element_type=F32
    )
    keep = lax.broadcasted_iota(jnp.int32, (4, LANES), 1) // 32 == lax.broadcasted_iota(jnp.int32, (4, LANES), 0)
    packed[0:1, :] = jnp.sum(jnp.where(keep, spread, 0.0), axis=0, keepdims=True)
    apart = lax.broadcasted_iota(jnp.int32, (4, LANES), 1) == 32 * lax.broadcasted_iota(jnp.int32, (4, LANES), 0)
    packed[1:2, :] = jnp.dot(
        skip_in[...], jnp.where(apart, 1.0, 0.0).astype(F32), precision=HIGHEST, preferred_element_type=F32
    )
    g_all[me] = packed[...]

    def weight(block):
        return w_ref[pl.ds(pl.multiple_of(block * 256, 256), 256), :]

    for load in loads[3:5]:
        load.wait()
    cot = cot_in[...]
    for h in range(2):
        zt = 1 - zh if h == 0 else zh
        for d in range(4):
            psend[h, pl.ds(d * CHUNK, CHUNK), :] = dot_nt(cot, weight(at(zt, ys[d], 1 - c)))
            pown[h, pl.ds(d * CHUNK, CHUNK), :] = dot_nt(cot, weight(at(zt, ys[d], c)))

    def tile(ref, step, g):
        return ref[g, pl.ds(step * 8, 8), :]

    def by_step(src, dst):
        for g in range(GROUPS):
            for step in range(STEPS):
                dst[g, pl.ds(step * 8, 8), :] = src[g, pl.ds(step, 8, stride=STEPS), :]

    loads[5].wait()
    for j, dst in enumerate((qs, ks, vs)):
        for g in range(GROUPS):
            turn[g] = qkv_in[j, pl.ds(g * LANES, LANES), :].astype(F32).T
        by_step(turn, dst)
    mix[...] = ks[...] * vs[...]
    pl.semaphore_wait(barrier, CTX - 1 + 5)

    core = [
        remote(psend.at[h], prx.at[h], sem_s.at[h], sem_r.at[h], tdev(zh, y, 1 - c)) for h in range(2)
    ]
    core[0].start()

    @pl.loop(1, CTX)
    def _(i):
        remote(packed, g_all.at[me], sem_s.at[2], sem_r.at[2], cdev(lax.rem(me + i, CTX))).start()

    core[1].start()
    sums = []
    for h in range(2):
        core[h].wait_recv()
        copies = []
        for d in (1, 2, 3):
            rows = pl.ds(d * CHUNK, CHUNK)
            ysend[h, d - 1] = pown[h, rows, :] + prx[h, rows, :]
            k = 4 + h * 3 + d - 1
            copy = remote(
                ysend.at[h, d - 1], yrx.at[h, d - 1], sem_s.at[k], sem_r.at[k], tdev(zh, ys[d], c)
            )
            copy.start()
            copies.append(copy)
        sums.append(copies)

    def summed(h):
        rows = pl.ds(0, CHUNK)
        total = pown[h, rows, :] + prx[h, rows, :]
        for d in range(3):
            sums[h][d].wait_recv()
            total = total + yrx[h, d]
        return total

    zsend[...] = summed(0)
    zcopy = remote(zsend, zrx, sem_s.at[10], sem_r.at[10], tdev(1 - zh, y, c))
    zcopy.start()
    pown[1, pl.ds(0, CHUNK), :] = summed(1)

    remote(g_all.at[pl.ds(0, CTX - 1)], g_all.at[pl.ds(0, CTX - 1)], sem_s.at[2], sem_r.at[2], cdev(me)).wait()
    for j in range(CTX):
        g_two[pl.ds(j, 1), :] = g_all[j, 0:1, :]
        g_two[pl.ds(CTX + j, 1), :] = g_all[j, 1:2, :]
    turned = g_two[...].T
    source = lax.broadcasted_iota(jnp.int32, (LANES, 512), 0)
    target = lax.broadcasted_iota(jnp.int32, (LANES, 512), 1)
    params = jnp.zeros((32, 512), F32)
    for i in range(4):
        place = jnp.where(target == source * 4 + i, 1.0, 0.0).astype(F32)
        params += jnp.dot(turned[i * 32 : i * 32 + 32, :], place, precision=HIGHEST, preferred_element_type=F32)
    sub = lax.broadcasted_iota(jnp.int32, (SUB, LANES), 0)
    subf = sub.astype(F32)
    for g in range(GROUPS):
        lanes = slice(g * LANES, (g + 1) * LANES)
        skip_t[pl.ds(g * 8, 8), :] = jnp.broadcast_to(params[0:1, 256 + g * LANES : 256 + (g + 1) * LANES], (8, LANES))
        for r in range(16):
            idx = r * 2 + g
            rows = pl.ds(idx * 8, 8)
            rate = jnp.broadcast_to(params[16 + r : 17 + r, lanes], (8, LANES)) * (-1.0 / SEQ)
            r_t[rows, :] = jnp.broadcast_to(params[r : r + 1, lanes], (8, LANES))
            a_t[rows, :] = jnp.exp(rate)
            a16_t[rows, :] = jnp.exp(rate * 16.0)
            f_t[rows, :] = jnp.exp(rate * (16.0 * subf))
            v_t[rows, :] = jnp.exp(rate * (16.0 * (7.0 - subf)))
            a128_t[pl.ds(idx, 1), :] = jnp.exp(rate[0:1, :] * 128.0)

    def rows_of(i, u, g):
        return pl.ds(pl.multiple_of(i * 64 + (u * 2 + g) * 8, 8), 8)

    def eight(i):
        return pl.ds(pl.multiple_of(i * 8, 8), 8)

    def collapse(x):
        return jnp.sum(x, axis=0, keepdims=True)

    mine = me // 16
    is_owner = lax.rem(me, 16) == 7 + lax.rem(mine, 2)

    def send_to_owner(o, src, dst, k):
        @pl.when(me != owner_of(o))
        def _():
            remote(src, dst, sem_s.at[k], sem_r.at[k], cdev(owner_of(o))).start()

        @pl.when(me == owner_of(o))
        def _():
            pltpu.make_async_copy(src, dst, sem_r.at[k]).start()

    def send_to_owners(tx, rx, rows, k):
        for o in range(OWNERS):
            send_to_owner(o, tx.at[pl.ds(o * rows, rows)], rx.at[pl.ds(pl.multiple_of(me * rows, 8), rows)], k)

    def wait_sent(ref, k):
        remote(ref, ref, sem_s.at[k], sem_r.at[k], cdev(me)).wait_send()

    def sent_to_owners(tx, rows, k):
        @pl.when(is_owner)
        def _():
            wait_sent(tx.at[pl.ds(0, 3 * rows)], k)

        @pl.when(jnp.logical_not(is_owner))
        def _():
            wait_sent(tx, k)

    def from_owner(source_of, dst, k):
        @pl.loop(0, CTX)
        def _(j):
            src = source_of(j)

            @pl.when(j != me)
            def _():
                remote(src, dst, sem_s.at[k], sem_r.at[k], cdev(j)).start()

            @pl.when(j == me)
            def _():
                pltpu.make_async_copy(src, dst, sem_r.at[k]).start()

    def wait_all(ref, k):
        remote(ref, ref, sem_s.at[k], sem_r.at[k], cdev(me)).wait_recv()

    @pl.loop(0, 4)
    def _(i):
        ends = []
        for u in range(4):
            for g in range(GROUPS):
                rows = rows_of(i, u, g)
                a = a_t[rows, :]
                s = tile(mix, 0, g)
                for step in range(1, STEPS):
                    s = a * s + tile(mix, step, g)
                ek_t[rows, :] = s
                ends.append(collapse(v_t[rows, :] * s))
        etx[eight(i), :] = jnp.concatenate(ends, axis=0)

    send_to_owners(etx, erx, OROWS, 11)

    @pl.when(is_owner)
    def _():
        decay = a128_t[eight(mine), :]
        wait_all(erx, 11)

        def forward(j, s):
            stx[eight(j), :] = s
            return decay * s + erx[eight(j), :]

        lax.fori_loop(0, CTX, forward, jnp.zeros((8, LANES), F32))
        from_owner(lambda j: stx.at[eight(j)], sin.at[eight(mine)], 13)

    zcopy.wait_recv()
    for g in range(GROUPS):
        lanes = pl.ds(g * LANES, LANES)
        turn[g] = pown[1, pl.ds(0, CHUNK), lanes] + zrx[:, lanes]
    by_step(turn, grad)
    gconv[...] = grad[...] * qs[...]

    @pl.loop(0, 4)
    def _(i):
        ends = []
        for u in range(4):
            for g in range(GROUPS):
                rows = rows_of(i, u, g)
                a = a_t[rows, :]
                b = tile(gconv, STEPS - 1, g)
                for step in range(STEPS - 2, -1, -1):
                    b = a * b + tile(gconv, step, g)
                bk_t[rows, :] = b
                ends.append(collapse(f_t[rows, :] * b))
        btx[eight(i), :] = jnp.concatenate(ends, axis=0)

    send_to_owners(btx, brx, OROWS, 12)
    for g in range(GROUPS):
        ktx[pl.ds(g, 1), :] = collapse(collapse(gconv[g] * mix[g]))
    send_to_owner(0, ktx, krx.at[me], 17)

    def starts(rows, ends_t, toward):
        x = ends_t[rows, :]
        a = a16_t[rows, :]
        for reach in (0, 1, 2, 4):
            shift = max(reach, 1)
            inside = sub >= shift if toward > 0 else sub < SUB - shift
            moved = jnp.where(inside, pltpu.roll(x, shift if toward > 0 else SUB - shift, 0), 0.0)
            if reach == 0:
                x = moved
            else:
                x = x + a * moved
                a = a * a
        return x

    for g in range(GROUPS):
        for step in range(STEPS):
            conv[g, pl.ds(step * 8, 8), :] = skip_t[pl.ds(g * 8, 8), :] * tile(mix, step, g)
    wait_all(sin, 13)

    @pl.loop(0, 4)
    def _(i):
        entering = sin[eight(i), :]
        for g in range(GROUPS):
            rows = [rows_of(i, u, g) for u in range(4)]
            s = [
                starts(rows[u], ek_t, 1) + f_t[rows[u], :] * entering[u * 2 + g : u * 2 + g + 1, :]
                for u in range(4)
            ]
            for u in range(4):
                ek_t[rows[u], :] = s[u]
            a = [a_t[rows[u], :] for u in range(4)]
            res = [r_t[rows[u], :] for u in range(4)]
            for step in range(STEPS):
                m = tile(mix, step, g)
                s = [a[u] * s[u] + m for u in range(4)]
                conv[g, pl.ds(step * 8, 8), :] += (res[0] * s[0] + res[1] * s[1]) + (res[2] * s[2] + res[3] * s[3])

    own = at(zh, y, c)
    for g in range(GROUPS):
        for step in range(STEPS):
            turn[g, pl.ds(step, 8, stride=STEPS), :] = tile(qs, step, g) * tile(conv, step, g)
        gall[own, :, pl.ds(g * LANES, LANES)] = turn[g].astype(BF16)

    started = []

    def pass_on(block, device):
        k = len(started)
        copy = remote(gall.at[block], gall.at[block], ag_s.at[k], ag_r.at[block], device)
        copy.start()
        started.append(copy)

    def arrived(block):
        remote(gall.at[block], gall.at[block], ag_s.at[0], ag_r.at[block], tdev(1 - zh, y, c)).wait_recv()

    pass_on(own, tdev(1 - zh, y, c))
    for d in (1, 2, 3):
        pass_on(own, tdev(zh, ys[d], c))
    pass_on(own, tdev(zh, y, 1 - c))

    @pl.loop(0, 4)
    def _(i):
        tiles = [[None] * 8 for _ in range(3)]
        for g in range(GROUPS):
            for u in range(4):
                rows = rows_of(i, u, g)
                a = a_t[rows, :]
                s = ek_t[rows, :]
                res_sum = jnp.zeros((8, LANES), F32)
                dec_sum = jnp.zeros((8, LANES), F32)
                cross = jnp.zeros((8, LANES), F32)
                before = []
                for step in range(STEPS):
                    p = a * s
                    before.append(p)
                    s = p + tile(mix, step, g)
                    res_sum = res_sum + tile(gconv, step, g) * s
                    cross = a * (cross + p)
                b = starts(rows, bk_t, -1)
                bk_t[rows, :] = b
                for step in range(STEPS - 1, -1, -1):
                    b = a * b + tile(gconv, step, g)
                    dec_sum = dec_sum + before[step] * b
                scale = r_t[rows, :] * (-1.0 / SEQ)
                tiles[g][u] = collapse(res_sum)
                tiles[g][4 + u] = collapse(dec_sum * scale)
                tiles[2][u * 2 + g] = collapse(cross * scale * v_t[rows, :])
        for n in range(3):
            gtx[pl.ds(pl.multiple_of(i * GROWS + n * 8, 8), 8), :] = jnp.concatenate(tiles[n], axis=0)

    send_to_owners(gtx, grx, GROWS, 15)

    @pl.when(is_owner)
    def _():
        decay = a128_t[eight(mine), :]
        wait_all(brx, 12)

        def backward(i, b):
            otx[eight(CTX - 1 - i), :] = b
            return decay * b + brx[eight(CTX - 1 - i), :]

        lax.fori_loop(0, CTX, backward, jnp.zeros((8, LANES), F32))
        from_owner(lambda j: otx.at[eight(j)], bin_.at[eight(mine)], 14)

    def project(block):
        return dot(gall[block], weight(block))

    def gather(half):
        zt = zh if half == 0 else 1 - zh
        for d in (1, 2, 3):
            block = at(zt, ys[d], c)
            arrived(block)
            pass_on(block, tdev(zh, y, 1 - c))
            out_ref[...] += project(block)
        for d in range(4):
            block = at(zt, ys[d], 1 - c)
            arrived(block)
            out_ref[...] += project(block)

    out_ref[...] = project(own)
    gather(0)
    block = at(1 - zh, y, c)
    arrived(block)
    for d in (1, 2, 3):
        pass_on(block, tdev(zh, ys[d], c))
    pass_on(block, tdev(zh, y, 1 - c))
    out_ref[...] += project(block)

    @pl.when(is_owner)
    def _():
        wait_all(grx, 15)

        def add(j, sums):
            at_ = lambda n: grx[pl.ds(pl.multiple_of(j * GROWS + n * 8, 8), 8), :]
            return sums[0] + at_(0), sums[1] + at_(1), sums[2] + at_(2) * otx[eight(j), :]

        zero = jnp.zeros((8, LANES), F32)
        total = lax.fori_loop(0, CTX, add, (zero, zero, zero))
        for g in range(GROUPS):
            joined = [zero[0:4]] + [total[2][u * 2 + g : u * 2 + g + 1] for u in range(4)]
            gsum[pl.ds(g * 8, 8), :] = total[g] + jnp.concatenate(joined, axis=0)
        from_owner(lambda j: gsum.at[eight(j // 32)], frx.at[eight(mine)], 16)

    @pl.when(me == owner_of(0))
    def _():
        wait_all(krx, 17)
        ksum[...] = lax.fori_loop(0, CTX, lambda j, s: s + krx[j], jnp.zeros((2, LANES), F32))
        from_owner(lambda j: ksum, kfin, 18)

    for g in range(GROUPS):
        for step in range(STEPS):
            back[g, pl.ds(step * 8, 8), :] = skip_t[pl.ds(g * 8, 8), :] * tile(gconv, step, g)
    wait_all(bin_, 14)

    @pl.loop(0, 4)
    def _(i):
        entering = bin_[eight(i), :]
        for g in range(GROUPS):
            rows = [rows_of(i, u, g) for u in range(4)]
            b = [bk_t[rows[u], :] + v_t[rows[u], :] * entering[u * 2 + g : u * 2 + g + 1, :] for u in range(4)]
            a = [a_t[rows[u], :] for u in range(4)]
            res = [r_t[rows[u], :] for u in range(4)]
            for step in range(STEPS - 1, -1, -1):
                gc = tile(gconv, step, g)
                b = [a[u] * b[u] + gc for u in range(4)]
                back[g, pl.ds(step * 8, 8), :] += (res[0] * b[0] + res[1] * b[1]) + (res[2] * b[2] + res[3] * b[3])

    for j, (left, right) in enumerate(((grad, conv), (back, vs), (back, ks))):
        for g in range(GROUPS):
            for step in range(STEPS):
                turn[g, pl.ds(step, 8, stride=STEPS), :] = tile(left, step, g) * tile(right, step, g)
            proj_ref[j, pl.ds(g * LANES, LANES), :] = turn[g].T

    gather(1)

    wait_all(frx, 16)
    wait_all(kfin, 18)
    chosen = lax.broadcasted_iota(jnp.int32, (8, LANES), 1) == lax.rem(me, 32) * 4 + lax.broadcasted_iota(
        jnp.int32, (8, LANES), 0
    )
    chosen = jnp.where(chosen, 1.0, 0.0).astype(F32)

    def pick(x):
        return lax.dot_general(
            chosen, x, (((1,), (1,)), ((), ())), precision=HIGHEST, preferred_element_type=F32
        )[0:4]

    res_ref[...] = pick(jnp.concatenate([frx[pl.ds(o * 8, 4), :] for o in range(OWNERS)], axis=0))
    dec_ref[...] = pick(jnp.concatenate([frx[pl.ds(o * 8 + 4, 4), :] for o in range(OWNERS)], axis=0))
    my_skip = jnp.where(me // 32 == 0, kfin[0:1, :], kfin[1:2, :])
    skip_ref[...] = lax.dot_general(
        my_skip, chosen, (((1,), (1,)), ((), ())), precision=HIGHEST, preferred_element_type=F32
    )[:, 0:4]

    for h in range(2):
        core[h].wait_send()
        for copy in sums[h]:
            copy.wait_send()
    zcopy.wait_send()
    for copy in started:
        copy.wait_send()
    sent_to_owners(etx, OROWS, 11)
    sent_to_owners(btx, OROWS, 12)
    sent_to_owners(gtx, GROWS, 15)

    @pl.when(is_owner)
    def _():
        for k in (13, 14, 16):
            wait_sent(stx.at[pl.ds(0, (CTX - 1) * OROWS)], k)

    @pl.when(me == owner_of(0))
    def _():
        wait_sent(krx.at[pl.ds(0, CTX - 1)], 18)

    @pl.when(me != owner_of(0))
    def _():
        wait_sent(ktx, 17)


def local(streams, out_weight, cotangent, residues, decay_rates, skip_gain):
    channels, width = streams.shape[0], out_weight.shape[1]
    vmem = pl.BlockSpec(memory_space=pltpu.VMEM)
    f, h = lambda *s: pltpu.VMEM(s, F32), lambda *s: pltpu.VMEM(s, BF16)
    block_out, proj, residue_grad, decay_grad, skip_grad = pl.pallas_call(
        kernel,
        name="hyena",
        out_shape=(
            jax.ShapeDtypeStruct((CHUNK, width), F32),
            jax.ShapeDtypeStruct((3, channels, CHUNK), F32),
            jax.ShapeDtypeStruct((4, 16), F32),
            jax.ShapeDtypeStruct((4, 16), F32),
            jax.ShapeDtypeStruct((1, 4), F32),
        ),
        in_specs=[pl.BlockSpec(memory_space=pl.ANY)] * 6,
        out_specs=(vmem,) * 5,
        scratch_shapes=[
            f(4, 16), f(4, 16), f(1, 4), h(3, 256, 128), h(128, 512), h(4096, 512),
            f(2, 128), f(CTX, 2, 128), f(128, 128), f(2, 512, 256), f(2, 512, 256), f(2, 512, 256),
            f(2, 3, 128, 256), f(2, 3, 128, 256), f(128, 256), f(128, 256),
            f(32, 128), f(512, 128), f(512, 128), f(32, 128),
            f(32, 128), f(512, 128), f(512, 128), f(32, 128),
            f(96, 128), f(CTX * GROWS, 128), f(16, 128), f(32, 128),
            f(2, 128), f(CTX, 2, 128), f(2, 128), f(2, 128),
            f(256, 128), f(256, 128), f(256, 128), f(256, 128), f(256, 128), f(256, 128), f(256, 128),
            f(32, 128), f(16, 128),
            f(2, 128, 128), f(2, 128, 128), f(2, 128, 128), f(2, 128, 128), f(2, 128, 128),
            f(2, 128, 128), f(2, 128, 128), f(2, 128, 128), f(2, 128, 128), h(16, 128, 256),
            pltpu.SemaphoreType.DMA((19,)), pltpu.SemaphoreType.DMA((19,)),
            pltpu.SemaphoreType.DMA((15,)), pltpu.SemaphoreType.DMA((16,)), pltpu.SemaphoreType.DMA((6,)),
        ],
        compiler_params=pltpu.CompilerParams(
            collective_id=0, has_side_effects=True, vmem_limit_bytes=60 * 2**20
        ),
    )(residues, decay_rates, skip_gain.reshape(1, 4), streams.transpose(1, 0, 2), cotangent, out_weight)
    return block_out, proj.transpose(1, 0, 2), residue_grad, decay_grad, skip_grad.reshape(4)


def solution(mesh):
    return jax.shard_map(
        local,
        mesh=mesh,
        in_specs=(
            P("tensor", None, "context"),
            P(None, "tensor"),
            P("context", "tensor"),
            P(("tensor", "context"), None),
            P(("tensor", "context"), None),
            P(("tensor", "context")),
        ),
        out_specs=(
            P("context", "tensor"),
            P("tensor", None, "context"),
            P(("tensor", "context"), None),
            P(("tensor", "context"), None),
            P(("tensor", "context")),
        ),
        check_vma=False,
    )
```
